256 devices in a mesh: dom: 128 (over x, z, y), col: 2 (over core).
Axes of the slice: x: 4, y: 4, z: 8, core: 2. Of those that a mesh axis runs over, the one named last changes fastest.
Arguments:
- first_interp: bfloat16 [8192, 4, 128, 128], P('dom'), may hold values from -0.25 to 0.25
- first_ids: int32 [8192, 4], P('dom'), may hold values from 0 to 7
- second_interp: bfloat16 [1024, 128, 1024], P('dom', None, 'col'), may hold values from -6 to 6
- coupling: bfloat16 [4096, 128, 128], P('dom'), may hold values from -0.25 to 0.25
- send_rows: int32 [512, 8], P('dom'), may hold values from 0 to 7, each once within a row
- targets: int32 [1024], P('dom'), may hold values from 0 to 63
- keep_mask: int32 [8192, 8], P('dom', 'col'), may hold values from 0 to 1, as said below
Outputs:
- interp: bfloat16 [8192, 128, 1024], P('dom', None, 'col')
The draws below stay inside these ranges and needn't reach their ends.
Inputs may be any that keep to these rules, and one draw needn't show every extreme that they name: `keep_mask`: every fine row block keeps at least one block of columns.
All inputs are finite; a program needn't handle non-finite values.
Results may differ from the reference program's by a relative error of at most 0.001.
Values may be sent and summed in bfloat16 or wider, within the bound.
No kernel may reach another device: no remote copies, remote signals or barrier semaphores. Data moves between devices by JAX's collectives and lax.ppermute only.
A program may use at most 192 MiB of HBM per device.

```python
import jax
import jax.numpy as jnp
from jax import lax

B = 128
NCOL = 1024
FB = 64
MB = 8
K1 = 4
BITS = 4
G = 4
TB = 2
NCB = 8
DOMS = 128
FINE_BLK = 8192
MID_BLK = 1024


def draw_keep_mask(key, part):
    key = jax.random.fold_in(key, 7)
    first_key, second_key = jax.random.split(key)
    levels = jax.random.randint(first_key, (FINE_BLK, NCB), 0, 4)
    chosen = jax.random.randint(second_key, (FINE_BLK, 1), 0, NCB)
    columns = jnp.arange(NCB, dtype=jnp.int32)[None, :]
    return jnp.where((levels > 0) | (columns == chosen), 1, 0).astype(jnp.int32)


def plant(values, own_key, least, top_value):
    extent = values.shape
    spot = [jax.random.randint(jax.random.fold_in(own_key, axis), (), 0, extent[axis]) for axis in range(len(extent))]
    values = values.at[tuple(spot)].set(least)
    longest = extent.index(max(extent))
    spot[longest] = (spot[longest] + 1) % extent[longest]
    return values.at[tuple(spot)].set(top_value)


def steps_of(key, dims, shards, least, largest):
    def one(dim, parts):
        steps = jax.random.uniform(jax.random.fold_in(jax.random.fold_in(key, 6), dim), (parts,), jnp.float32, least / len(shards), largest / len(shards))
        return jnp.repeat(jnp.exp(steps), dims[dim] // parts).reshape((-1,) + (1,) * (len(dims) - dim - 1))

    level = one(*shards[0])
    for cut in shards[1:]:
        level = level * one(*cut)
    return level


def normal_values(own_key, extent, spread, most, cuts=(), held_as=jnp.bfloat16):
    level = steps_of(own_key, extent, cuts, -0.22, 0.18) if cuts else 1.0
    values = jax.random.normal(own_key, extent, jnp.float32) * spread * level
    return jnp.minimum(jnp.maximum(values, -most), most).astype(held_as)


def setup_inputs(seed: int = 0) -> dict:
    seeds = jax.random.split(jax.random.key(seed), 8)
    return {
        "first_interp": normal_values(seeds[0], (FINE_BLK, K1, B, B), (K1 * B) ** -0.5, 0.25, ((0, 128),)),
        "first_ids": plant(jax.random.randint(seeds[1], (FINE_BLK, K1), 0, MB), jax.random.fold_in(seeds[1], 1), 0, MB - 1).astype(jnp.int32),
        "second_interp": normal_values(seeds[2], (MID_BLK, B, NCOL), 1.0, 6.0, ((0, 128), (2, 2))),
        "coupling": normal_values(seeds[3], (DOMS * BITS * MB, B, B), (K1 * B) ** -0.5, 0.25, ((0, 128),)),
        "send_rows": jax.vmap(lambda own: jax.random.permutation(own, MB))(jax.random.split(seeds[4], (DOMS * BITS))).reshape((DOMS * BITS, MB)).astype(jnp.int32),
        "targets": plant(jax.random.randint(seeds[5], (DOMS * BITS * TB,), 0, FB), jax.random.fold_in(seeds[5], 1), 0, FB - 1).astype(jnp.int32),
        "keep_mask": draw_keep_mask(jax.random.fold_in(seeds[7], 71), 0),
    }


epsilon = 1e-6


def finish(raw, masks):
    magnitude = jnp.abs(raw)
    weights = masks.astype(jnp.float32)[:, None, :, None]
    full = jnp.sum(magnitude, axis=2)
    kept = jnp.sum(magnitude.reshape(FB, B, NCB, B) * weights, axis=(2, 3))
    scale = full / (kept + epsilon)
    kept_raw = (raw.reshape(FB, B, NCB, B) * weights).reshape(FB, B, NCOL)
    return (kept_raw * scale[:, :, None]).astype(jnp.bfloat16)


def reference(first_interp, first_ids, second_interp, coupling, send_rows, targets, keep_mask):
    first_all = first_interp.reshape(DOMS, FB, K1, B, B)
    ids_all = first_ids.reshape(DOMS, FB, K1)
    second_all = second_interp.reshape(DOMS, MB, B, NCOL)
    coupling_all = coupling.reshape(DOMS, BITS, MB, B, B)
    sends_all = send_rows.reshape(DOMS, BITS, MB)
    targets_all = targets.reshape(DOMS, BITS, TB)
    masks_all = keep_mask.reshape(DOMS, FB, NCB)

    def per_domain(domain):
        own_rows = second_all[domain]
        gathered = own_rows[ids_all[domain]].astype(jnp.float32)
        raw = jnp.einsum("fkab,fkbn->fan", first_all[domain].astype(jnp.float32), gathered)
        for bit_level in range(BITS):
            partner = jnp.bitwise_xor(domain, 1 << bit_level)
            rows = second_all[partner][sends_all[partner, bit_level]].astype(jnp.float32)
            products = jnp.einsum("sab,sbn->san", coupling_all[domain, bit_level].astype(jnp.float32), rows)
            grouped = jnp.sum(products.reshape(TB, G, B, NCOL), axis=1)
            raw = raw.at[targets_all[domain, bit_level]].add(grouped)
        return finish(raw, masks_all[domain])

    result = lax.map(per_domain, jnp.arange(DOMS, dtype=jnp.int32))
    return result.reshape(FINE_BLK, B, NCOL)
```

```python
import functools

import jax
import jax.numpy as jnp
from jax import lax
from jax.experimental import pallas as pl
from jax.experimental.pallas import tpu as pltpu
from jax.sharding import PartitionSpec as P

G = 4
LEVELS = 4
GROUPS = 2
CHUNK = 8
WAVES = ((3, 1), (0, 2))
epsilon = 1e-06
VMEM_SCOPED = 14 * 2**20
SMEM_SPEC = pl.BlockSpec(memory_space=pltpu.SMEM)
VMEM_SPEC = pl.BlockSpec(memory_space=pltpu.VMEM)
HBM_SPEC = pl.BlockSpec(memory_space=pltpu.HBM)
ANY_SPEC = pl.BlockSpec(memory_space=pl.ANY)


def lanes():
    return lax.broadcasted_iota(jnp.int32, (128, 128), 1)


def level_of(wave, core):
    first, second = WAVES[wave]
    return jnp.where(core == 0, first, second)


def row_sums(block, weights):
    full = kept = None
    for column in range(4):
        part = jnp.abs(block[:, column * 128 : (column + 1) * 128])
        weighted = part * weights[column]
        full = part if full is None else full + part
        kept = weighted if kept is None else kept + weighted
    return jnp.sum(full, axis=1, keepdims=True), jnp.sum(kept, axis=1, keepdims=True)


def weights_of(mask, block):
    return [mask[column, block].astype(jnp.float32) for column in range(4)]


def inner_block(ids, mask, block, first, second, raw, sums):
    left = jnp.concatenate([first[k] for k in range(4)], axis=1)
    right = jnp.concatenate([second[ids[k, block]] for k in range(4)], axis=0)
    product = jnp.dot(left, right, preferred_element_type=jnp.float32)
    raw[block] = product
    full, kept = row_sums(product, weights_of(mask, block))
    lane = lanes()
    sums[...] = jnp.where(lane == block, full, jnp.where(lane == block + 64, kept, sums[...]))


def pick_level(wave, by_level, out, sem):
    copy = pltpu.make_async_copy(by_level.at[level_of(wave, lax.axis_index("col"))], out, sem)
    copy.start()
    copy.wait()


def inner_head(
    count, tables_hbm, first_hbm, second_hbm, tables, raw, sums, rest, second, head, table_sem, first_sem, rest_sem, second_sem
):
    total = first_hbm.shape[0]
    ids, mask = tables[:2]
    table_copies = [
        pltpu.make_async_copy(source, target, table_sem.at[place])
        for place, (source, target) in enumerate(zip(tables_hbm, tables))
    ]
    for copy in table_copies:
        copy.start()

    def first_copy(chunk):
        span = pl.ds(chunk * CHUNK, CHUNK)
        return pltpu.make_async_copy(first_hbm.at[span], head.at[span], first_sem.at[chunk])

    rest_copy = pltpu.make_async_copy(first_hbm.at[pl.ds(count, total - count)], rest, rest_sem)
    second_copy = pltpu.make_async_copy(second_hbm, second, second_sem)
    second_copy.start()
    for chunk in range(count // CHUNK):
        first_copy(chunk).start()
    rest_copy.start()
    sums[...] = jnp.zeros_like(sums)
    for copy in table_copies:
        copy.wait()
    second_copy.wait()

    @pl.loop(0, count // CHUNK)
    def _(chunk):
        first_copy(chunk).wait()
        for j in range(CHUNK):
            block = chunk * CHUNK + j
            inner_block(ids, mask, block, head.at[block], second, raw, sums)

    rest_copy.wait()


def inner_rest(start, ids, mask, rest, second, raw_in, sums_in, after, raw, sums):
    del raw_in, after
    sums[...] = sums_in[...]

    @pl.loop(0, rest.shape[0] // CHUNK)
    def _(chunk):
        for j in range(CHUNK):
            place = chunk * CHUNK + j
            inner_block(ids, mask, start + place, rest.at[place], second, raw, sums)


def coupling_products(wave, send_rows, tiles, second, second_other, after, out_own, out_other):
    del after
    level = level_of(wave, lax.axis_index("col"))
    for group in range(GROUPS):
        left = jnp.concatenate([tiles[group * G + s] for s in range(G)], axis=1)
        for rows, out in ((second, out_own), (second_other, out_other)):
            right = jnp.concatenate([rows[send_rows[level, group * G + s]] for s in range(G)], axis=0)
            product = jnp.dot(left, right, preferred_element_type=jnp.float32)
            top = jnp.max(jnp.abs(product), axis=1, keepdims=True)
            power = jnp.floor(jnp.log(jnp.maximum(top, 2.0**-100)) * 1.4426950408889634) + 1.0
            scaled = jnp.round(product * jnp.exp2(15.0 - power))
            coded = jnp.clip(scaled, -32767.0, 32767.0).astype(jnp.int32).astype(jnp.int16)
            for column in range(4):
                out[pl.ds((group * 4 + column) * 128, 128), :] = coded[:, column * 128 : (column + 1) * 128]
            turned = jnp.broadcast_to(power, (128, 128)).T
            out[pl.ds(1024 + 16 * group, 16), :] = turned[:16].astype(jnp.int32).astype(jnp.int16)


def scale_all(mask, raw, sums, sums_other, out_hbm, done, out, sem):
    done[...] = jnp.zeros_like(done)
    both = sums[...] + sums_other[...]
    scale = both[:, :64] / (both[:, 64:] + epsilon)
    scale = jnp.concatenate([scale, scale], axis=1)

    def out_copy(chunk):
        span = pl.ds(chunk * CHUNK, CHUNK)
        return pltpu.make_async_copy(out.at[span], out_hbm.at[span], sem.at[chunk])

    chunks = raw.shape[0] // CHUNK

    @pl.loop(0, chunks)
    def _(chunk):
        for j in range(CHUNK):
            block = chunk * CHUNK + j
            factor = jnp.take_along_axis(scale, jnp.full((128, 128), block, jnp.int32), axis=1)
            weights = weights_of(mask, block)
            for column in range(4):
                span = slice(column * 128, (column + 1) * 128)
                out[block, :, span] = (raw[block, :, span] * (factor * weights[column])).astype(jnp.bfloat16)
        out_copy(chunk).start()

    for chunk in range(chunks):
        out_copy(chunk).wait()


def add_products(targets, mask, raw_in, same_a, cross_a, same_b, cross_b, after, raw, final, sums):
    del raw_in, after
    core = lax.axis_index("col")
    for place, source in enumerate((same_a, cross_a, same_b, cross_b)):
        level = level_of(place // 2, core if place % 2 == 0 else 1 - core)
        for group in range(GROUPS):
            block = targets[level * GROUPS + group]
            power = source[pl.ds(1024 + 16 * group, 16), :].astype(jnp.int32).astype(jnp.float32)
            step = jnp.exp2(jnp.concatenate([power] * 8, axis=0).T - 15.0)
            for column in range(4):
                span = slice(column * 128, (column + 1) * 128)
                coded = source[pl.ds((group * 4 + column) * 128, 128), :].astype(jnp.int32)
                raw[block, :, span] += coded.astype(jnp.float32) * step
    lane = lanes()
    found = jnp.zeros((128, 128), jnp.float32)
    for entry in range(LEVELS * GROUPS):
        block = targets[entry]
        weights = weights_of(mask, block)
        product = raw[block]
        full, kept = row_sums(product, weights)
        found = jnp.where(lane == entry, full, jnp.where(lane == entry + 64, kept, found))
        for column in range(4):
            span = slice(column * 128, (column + 1) * 128)
            final[entry, :, span] = product[:, span] * weights[column]
    sums[...] = found


def scale_final(targets, final, sums, sums_other, out_in, out_hbm, out, sem):
    del out_in
    both = sums[...] + sums_other[...]
    scale = both[:, :64] / (both[:, 64:] + epsilon)
    blocks = [targets[entry] for entry in range(LEVELS * GROUPS)]
    latest = []
    for entry, block in enumerate(blocks):
        again = jnp.bool_(False)
        for later in blocks[entry + 1 :]:
            again = again | (later == block)
        latest.append(jnp.logical_not(again))

    def out_copy(entry):
        return pltpu.make_async_copy(out.at[entry], out_hbm.at[blocks[entry]], sem.at[entry])

    for entry in range(LEVELS * GROUPS):
        factor = jnp.broadcast_to(scale[:, entry : entry + 1], (128, 128))
        for column in range(4):
            span = slice(column * 128, (column + 1) * 128)
            out[entry, :, span] = (final[entry, :, span] * factor).astype(jnp.bfloat16)
        pl.when(latest[entry])(lambda entry=entry: out_copy(entry).start())
    for entry in range(LEVELS * GROUPS):
        pl.when(latest[entry])(lambda entry=entry: out_copy(entry).wait())


def call(kernel, name, outs, in_specs, out_specs, scratch=(), aliases=None):
    return pl.pallas_call(
        kernel,
        out_shape=outs,
        in_specs=in_specs,
        out_specs=out_specs,
        scratch_shapes=list(scratch),
        input_output_aliases=aliases or {},
        compiler_params=pltpu.CompilerParams(vmem_limit_bytes=VMEM_SCOPED),
        cost_estimate=pl.CostEstimate(flops=1, bytes_accessed=1, transcendentals=0),
        name=name,
    )


def route(count, wave, swap):
    pairs = []
    for domain in range(count):
        for core in range(2):
            other = domain ^ (1 << WAVES[wave][core])
            pairs.append((domain * 2 + core, other * 2 + (core ^ swap)))
    return pairs


def in_hbm(array):
    return pltpu.with_memory_space_constraint(array, pltpu.HBM)


def swap_cores(block):
    return lax.ppermute(block, "col", [(0, 1), (1, 0)])


def on_device(first_interp, first_ids, second_interp, coupling, send_rows, targets, keep_mask):
    fine = first_interp.shape[0]
    head = 24
    core = lax.axis_index("col")
    count = lax.axis_size("dom")
    by_level = in_hbm(coupling.reshape(LEVELS, 8, 128, 128))
    tiles = []
    for wave in range(2):
        own = call(
            functools.partial(pick_level, wave),
            "pick_level",
            pltpu.VMEM((8, 128, 128), jnp.bfloat16),
            [HBM_SPEC],
            VMEM_SPEC,
            [pltpu.SemaphoreType.DMA],
        )(by_level)
        tiles.append(lax.ppermute(own, ("dom", "col"), route(count, wave, 0)))
    second_other = swap_cores(second_interp)

    tables = [in_hbm(x) for x in (first_ids.T, keep_mask.T, send_rows, targets)]
    raw_shape = pltpu.VMEM((fine, 128, 512), jnp.float32)
    sums_shape = pltpu.VMEM((128, 128), jnp.float32)
    tables, raw, sums, rest, second = call(
        functools.partial(inner_head, head),
        "inner_head",
        (
            [pltpu.SMEM(x.shape, x.dtype) for x in tables],
            raw_shape,
            sums_shape,
            pltpu.VMEM((fine - head, 4, 128, 128), jnp.bfloat16),
            pltpu.VMEM((8, 128, 512), jnp.bfloat16),
        ),
        [[HBM_SPEC] * 4, HBM_SPEC, HBM_SPEC],
        ([SMEM_SPEC] * 4,) + (VMEM_SPEC,) * 4,
        [
            pltpu.VMEM((head, 4, 128, 128), jnp.bfloat16),
            pltpu.SemaphoreType.DMA((4,)),
            pltpu.SemaphoreType.DMA((head // CHUNK,)),
            pltpu.SemaphoreType.DMA,
            pltpu.SemaphoreType.DMA,
        ],
    )(tables, in_hbm(first_interp), in_hbm(second_interp))
    ids, mask, send_rows, targets = tables

    def products(wave, after):
        return call(
            functools.partial(coupling_products, wave),
            "coupling_products",
            (pltpu.VMEM((1056, 128), jnp.int16),) * 2,
            [SMEM_SPEC, VMEM_SPEC, VMEM_SPEC, VMEM_SPEC, ANY_SPEC],
            (VMEM_SPEC,) * 2,
        )(send_rows, tiles[wave], second, second_other, after)

    def deliver(wave, own, other):
        return (
            lax.ppermute(own, ("dom", "col"), route(count, wave, 0)),
            lax.ppermute(other, ("dom", "col"), route(count, wave, 1)),
        )

    own_a, other_a = products(0, sums)
    same_a, cross_a = deliver(0, own_a, other_a)
    own_b, other_b = products(1, own_a)
    same_b, cross_b = deliver(1, own_b, other_b)

    raw, sums = call(
        functools.partial(inner_rest, head),
        "inner_rest",
        (raw_shape, sums_shape),
        [SMEM_SPEC, SMEM_SPEC, VMEM_SPEC, VMEM_SPEC, VMEM_SPEC, VMEM_SPEC, ANY_SPEC],
        (VMEM_SPEC,) * 2,
        aliases={4: 0, 5: 1},
    )(ids, mask, rest, second, raw, sums, own_b)

    out, done = call(
        scale_all,
        "scale_all",
        (jax.ShapeDtypeStruct((fine, 128, 512), jnp.bfloat16), pltpu.VMEM((8, 128), jnp.float32)),
        [SMEM_SPEC, VMEM_SPEC, VMEM_SPEC, VMEM_SPEC],
        (HBM_SPEC, VMEM_SPEC),
        [pltpu.VMEM((fine, 128, 512), jnp.bfloat16), pltpu.SemaphoreType.DMA((fine // CHUNK,))],
    )(mask, raw, sums, swap_cores(sums))

    _, final, sums = call(
        add_products,
        "add_products",
        (raw_shape, pltpu.VMEM((8, 128, 512), jnp.float32), sums_shape),
        [SMEM_SPEC, SMEM_SPEC] + [VMEM_SPEC] * 6,
        (VMEM_SPEC,) * 3,
        aliases={2: 0},
    )(targets, mask, raw, same_a, cross_a, same_b, cross_b, done)
    return call(
        scale_final,
        "scale_final",
        jax.ShapeDtypeStruct((fine, 128, 512), jnp.bfloat16),
        [SMEM_SPEC, VMEM_SPEC, VMEM_SPEC, VMEM_SPEC, HBM_SPEC],
        HBM_SPEC,
        [pltpu.VMEM((8, 128, 512), jnp.bfloat16), pltpu.SemaphoreType.DMA((8,))],
        aliases={4: 0},
    )(targets, final, sums, swap_cores(sums), out)


def solution(mesh):
    return jax.shard_map(
        on_device,
        mesh=mesh,
        in_specs=(
            P("dom", None, None, None),
            P("dom", None),
            P("dom", None, "col"),
            P("dom", None, None),
            P("dom", None),
            P("dom"),
            P("dom", "col"),
        ),
        out_specs=P("dom", None, "col"),
        check_vma=False,
    )
```

```python
import functools

import jax
import jax.numpy as jnp
from jax import lax
from jax.experimental import pallas as pl
from jax.experimental.pallas import tpu as pltpu
from jax.sharding import PartitionSpec as P

G = 4
LEVELS = 4
GROUPS = 2
CHUNK = 8
WAVES = ((3, 1), (0, 2))
COSTS = dict(products0=1, products1=1, inner8=1, inner32=1, scale0=1, first=1, last=1)
epsilon = 1e-06
VMEM_SCOPED = 14 * 2**20
SMEM_SPEC = pl.BlockSpec(memory_space=pltpu.SMEM)
VMEM_SPEC = pl.BlockSpec(memory_space=pltpu.VMEM)
HBM_SPEC = pl.BlockSpec(memory_space=pltpu.HBM)
ANY_SPEC = pl.BlockSpec(memory_space=pl.ANY)


def lanes():
    return lax.broadcasted_iota(jnp.int32, (128, 128), 1)


def level_of(wave, core):
    first, second = WAVES[wave]
    return jnp.where(core == 0, first, second)


def row_sums(block, weights):
    full = kept = None
    for column in range(4):
        part = jnp.abs(block[:, column * 128 : (column + 1) * 128])
        weighted = part * weights[column]
        full = part if full is None else full + part
        kept = weighted if kept is None else kept + weighted
    return jnp.sum(full, axis=1, keepdims=True), jnp.sum(kept, axis=1, keepdims=True)


def weights_of(mask, block):
    return [mask[column, block].astype(jnp.float32) for column in range(4)]


def inner_block(ids, mask, block, first, second, raw, sums):
    left = jnp.concatenate([first[k] for k in range(4)], axis=1)
    right = jnp.concatenate([second[ids[k, block]] for k in range(4)], axis=0)
    product = jnp.dot(left, right, preferred_element_type=jnp.float32)
    raw[block] = product
    full, kept = row_sums(product, weights_of(mask, block))
    lane = lanes()
    sums[...] = jnp.where(lane == block, full, jnp.where(lane == block + 64, kept, sums[...]))


def tile_copy(wave, by_level, out, sem):
    return pltpu.make_async_copy(by_level.at[level_of(wave, lax.axis_index("col"))], out, sem)


def pick_tiles(by_level, out, sem):
    copy = tile_copy(0, by_level, out, sem)
    copy.start()
    copy.wait()


def inner_head(
    count,
    tables_hbm,
    first_hbm,
    second_hbm,
    by_level,
    after,
    tables,
    raw,
    sums,
    second,
    tiles_b,
    first,
    table_sem,
    first_sem,
    second_sem,
    tile_sem,
):
    del after
    ids, mask = tables[:2]
    copies = [pltpu.make_async_copy(second_hbm, second, second_sem)]
    for place, (source, target) in enumerate(zip(tables_hbm, tables)):
        copies.append(pltpu.make_async_copy(source, target, table_sem.at[place]))
    copies.append(pltpu.make_async_copy(first_hbm.at[pl.ds(0, count)], first, first_sem))
    copies.append(tile_copy(1, by_level, tiles_b, tile_sem))
    for copy in copies:
        copy.start()
    sums[...] = jnp.zeros_like(sums)
    for copy in copies:
        copy.wait()

    @pl.loop(0, count // CHUNK)
    def _(chunk):
        for j in range(CHUNK):
            block = chunk * CHUNK + j
            inner_block(ids, mask, block, first.at[block], second, raw, sums)


def inner_rest(start, count, fresh, ids, mask, first, second, raw_in, sums_in, after, raw, sums, done):
    del raw_in, after
    done[...] = jnp.zeros_like(done)
    sums[...] = jnp.zeros_like(sums) if fresh else sums_in[...]

    @pl.loop(0, count // CHUNK)
    def _(chunk):
        for j in range(CHUNK):
            block = start + chunk * CHUNK + j
            inner_block(ids, mask, block, first.at[block], second, raw, sums)


def coupling_products(wave, send_rows, tiles, second, second_other, after, out_own, out_other):
    del after
    level = level_of(wave, lax.axis_index("col"))
    for group in range(GROUPS):
        left = jnp.concatenate([tiles[group * G + s] for s in range(G)], axis=1)
        for rows, out in ((second, out_own), (second_other, out_other)):
            right = jnp.concatenate([rows[send_rows[level, group * G + s]] for s in range(G)], axis=0)
            product = jnp.dot(left, right, preferred_element_type=jnp.float32)
            top = jnp.max(jnp.abs(product), axis=1, keepdims=True)
            power = jnp.floor(jnp.log(jnp.maximum(top, 2.0**-100)) * 1.4426950408889634) + 1.0
            scaled = jnp.round(product * jnp.exp2(15.0 - power))
            coded = jnp.clip(scaled, -32767.0, 32767.0).astype(jnp.int32).astype(jnp.int16)
            for column in range(4):
                out[pl.ds((group * 4 + column) * 128, 128), :] = coded[:, column * 128 : (column + 1) * 128]
            turned = jnp.broadcast_to(power, (128, 128)).T
            out[pl.ds(1024 + 16 * group, 16), :] = turned[:16].astype(jnp.int32).astype(jnp.int16)


def scale_part(start, mask, raw, sums, sums_other, out_in, after, out_hbm, done, out, sem):
    del out_in, after
    done[...] = jnp.zeros_like(done)
    both = sums[...] + sums_other[...]
    scale = both[:, :64] / (both[:, 64:] + epsilon)
    scale = jnp.concatenate([scale, scale], axis=1)

    def out_copy(chunk):
        span = pl.ds(chunk * CHUNK, CHUNK)
        return pltpu.make_async_copy(out.at[span], out_hbm.at[pl.ds(start + chunk * CHUNK, CHUNK)], sem.at[chunk])

    chunks = out.shape[0] // CHUNK

    @pl.loop(0, chunks)
    def _(chunk):
        for j in range(CHUNK):
            place = chunk * CHUNK + j
            block = start + place
            factor = jnp.take_along_axis(scale, jnp.full((128, 128), block, jnp.int32), axis=1)
            weights = weights_of(mask, block)
            for column in range(4):
                span = slice(column * 128, (column + 1) * 128)
                out[place, :, span] = (raw[block, :, span] * (factor * weights[column])).astype(jnp.bfloat16)
        out_copy(chunk).start()

    for chunk in range(chunks):
        out_copy(chunk).wait()


def add_part(targets, level, group, source, part, raw):
    block = targets[level * GROUPS + group]
    power = source[pl.ds(1024 + 16 * part, 16), :].astype(jnp.int32).astype(jnp.float32)
    step = jnp.exp2(jnp.concatenate([power] * 8, axis=0).T - 15.0)
    for column in range(4):
        span = slice(column * 128, (column + 1) * 128)
        coded = source[pl.ds((part * 4 + column) * 128, 128), :].astype(jnp.int32)
        raw[block, :, span] += coded.astype(jnp.float32) * step


def add_wave(wave, targets, same, cross, raw):
    core = lax.axis_index("col")
    for group in range(GROUPS):
        add_part(targets, level_of(wave, core), group, same, group, raw)
        add_part(targets, level_of(wave, 1 - core), group, cross, group, raw)


def add_first(targets, raw_in, same, cross, after, raw):
    del raw_in, after
    add_wave(0, targets, same, cross, raw)


def add_last(targets, mask, raw_in, same, cross, raw, final, sums):
    del raw_in
    add_wave(1, targets, same, cross, raw)
    lane = lanes()
    found = jnp.zeros((128, 128), jnp.float32)
    for entry in range(LEVELS * GROUPS):
        block = targets[entry]
        weights = weights_of(mask, block)
        product = raw[block]
        full, kept = row_sums(product, weights)
        found = jnp.where(lane == entry, full, jnp.where(lane == entry + 64, kept, found))
        for column in range(4):
            span = slice(column * 128, (column + 1) * 128)
            final[entry, :, span] = product[:, span] * weights[column]
    sums[...] = found


def scale_final(targets, final, sums, sums_other, out_in, out_hbm, out, sem):
    del out_in
    both = sums[...] + sums_other[...]
    scale = both[:, :64] / (both[:, 64:] + epsilon)
    blocks = [targets[entry] for entry in range(LEVELS * GROUPS)]
    latest = []
    for entry, block in enumerate(blocks):
        again = jnp.bool_(False)
        for later in blocks[entry + 1 :]:
            again = again | (later == block)
        latest.append(jnp.logical_not(again))

    def out_copy(entry):
        return pltpu.make_async_copy(out.at[entry], out_hbm.at[blocks[entry]], sem.at[entry])

    for entry in range(LEVELS * GROUPS):
        factor = jnp.broadcast_to(scale[:, entry : entry + 1], (128, 128))
        for column in range(4):
            span = slice(column * 128, (column + 1) * 128)
            out[entry, :, span] = (final[entry, :, span] * factor).astype(jnp.bfloat16)
        pl.when(latest[entry])(lambda entry=entry: out_copy(entry).start())
    for entry in range(LEVELS * GROUPS):
        pl.when(latest[entry])(lambda entry=entry: out_copy(entry).wait())


def call(kernel, name, outs, in_specs, out_specs, scratch=(), aliases=None, flops=1):
    return pl.pallas_call(
        kernel,
        out_shape=outs,
        in_specs=in_specs,
        out_specs=out_specs,
        scratch_shapes=list(scratch),
        input_output_aliases=aliases or {},
        compiler_params=pltpu.CompilerParams(vmem_limit_bytes=VMEM_SCOPED),
        cost_estimate=pl.CostEstimate(flops=flops, bytes_accessed=1, transcendentals=0),
        name=name,
    )


def route(count, wave, swap):
    pairs = []
    for domain in range(count):
        for core in range(2):
            other = domain ^ (1 << WAVES[wave][core])
            pairs.append((domain * 2 + core, other * 2 + (core ^ swap)))
    return pairs


def in_hbm(array):
    return pltpu.with_memory_space_constraint(array, pltpu.HBM)


def in_vmem(array):
    return pltpu.with_memory_space_constraint(array, pltpu.VMEM)


def swap_cores(block):
    return lax.ppermute(block, "col", [(0, 1), (1, 0)])


def on_device(first_interp, first_ids, second_interp, coupling, send_rows, targets, keep_mask):
    fine = first_interp.shape[0]
    cuts = 8, 32
    count = lax.axis_size("dom")
    token = pltpu.VMEM((8, 128), jnp.float32)
    raw_shape = pltpu.VMEM((fine, 128, 512), jnp.float32)
    sums_shape = pltpu.VMEM((128, 128), jnp.float32)

    by_level = in_hbm(coupling.reshape(LEVELS, 8, 128, 128))
    tile_shape = pltpu.VMEM((8, 128, 128), jnp.bfloat16)
    tiles_a = call(pick_tiles, "pick_tiles", tile_shape, [HBM_SPEC], VMEM_SPEC, [pltpu.SemaphoreType.DMA])(by_level)
    second_other = swap_cores(second_interp)

    first = in_vmem(first_interp)
    tables = [in_hbm(x) for x in (first_ids.T, keep_mask.T, send_rows, targets)]
    head = cuts[0]
    tables, raw, sums, second, tiles_b = call(
        functools.partial(inner_head, head),
        "inner_head",
        (
            [pltpu.SMEM(x.shape, x.dtype) for x in tables],
            raw_shape,
            sums_shape,
            pltpu.VMEM((8, 128, 512), jnp.bfloat16),
            tile_shape,
        ),
        [[HBM_SPEC] * 4, HBM_SPEC, HBM_SPEC, HBM_SPEC, VMEM_SPEC],
        ([SMEM_SPEC] * 4,) + (VMEM_SPEC,) * 4,
        [
            pltpu.VMEM((head, 4, 128, 128), jnp.bfloat16),
            pltpu.SemaphoreType.DMA((4,)),
            pltpu.SemaphoreType.DMA,
            pltpu.SemaphoreType.DMA,
            pltpu.SemaphoreType.DMA,
        ],
    )(tables, in_hbm(first_interp), in_hbm(second_interp), by_level, tiles_a)
    came = [
        lax.ppermute(own, ("dom", "col"), route(count, wave, 0)) for wave, own in enumerate((tiles_a, tiles_b))
    ]
    ids, mask, send_rows, targets = tables

    def inner_part(start, stop, raw, sums, after, fresh=False):
        return call(
            functools.partial(inner_rest, start, stop - start, fresh),
            "inner_rest",
            (raw_shape, sums_shape, token),
            [SMEM_SPEC, SMEM_SPEC, VMEM_SPEC, VMEM_SPEC, VMEM_SPEC, VMEM_SPEC, VMEM_SPEC],
            (VMEM_SPEC,) * 3,
            aliases={4: 0} if fresh else {4: 0, 5: 1},
            flops=COSTS[f"inner{start}"],
        )(ids, mask, first, second, raw, sums, after)

    def products(wave, after):
        outs = call(
            functools.partial(coupling_products, wave),
            "coupling_products",
            (pltpu.VMEM((1056, 128), jnp.int16),) * 2,
            [SMEM_SPEC, VMEM_SPEC, VMEM_SPEC, VMEM_SPEC, VMEM_SPEC],
            (VMEM_SPEC,) * 2,
            flops=COSTS[f"products{wave}"],
        )(send_rows, came[wave], second, second_other, after)
        return outs, [lax.ppermute(x, ("dom", "col"), route(count, wave, swap)) for swap, x in enumerate(outs)]

    def scaled(start, stop, sums, out, after):
        return call(
            functools.partial(scale_part, start),
            "scale_part",
            (jax.ShapeDtypeStruct((fine, 128, 512), jnp.bfloat16), token),
            [SMEM_SPEC, VMEM_SPEC, VMEM_SPEC, VMEM_SPEC, HBM_SPEC if start else VMEM_SPEC, VMEM_SPEC],
            (HBM_SPEC, VMEM_SPEC),
            [pltpu.VMEM((stop - start, 128, 512), jnp.bfloat16), pltpu.SemaphoreType.DMA(((stop - start) // CHUNK,))],
            aliases={4: 0} if start else None,
            flops=COSTS[f"scale{start}"],
        )(mask, raw, sums, swap_cores(sums), out, after)

    raw, sums, done = inner_part(cuts[0], cuts[1], raw, sums, second)
    outs, (same_a, cross_a) = products(0, done)
    outs, (same_b, cross_b) = products(1, outs[0])
    raw, sums, done = inner_part(cuts[1], fine, raw, sums, outs[0])
    out, done = scaled(0, fine, sums, done, done)
    raw = call(
        add_first,
        "add_first",
        raw_shape,
        [SMEM_SPEC] + [VMEM_SPEC] * 4,
        VMEM_SPEC,
        aliases={1: 0},
        flops=COSTS["first"],
    )(targets, raw, same_a, cross_a, done)
    _, final, sums = call(
        add_last,
        "add_last",
        (raw_shape, pltpu.VMEM((8, 128, 512), jnp.float32), sums_shape),
        [SMEM_SPEC, SMEM_SPEC] + [VMEM_SPEC] * 3,
        (VMEM_SPEC,) * 3,
        aliases={2: 0},
        flops=COSTS["last"],
    )(targets, mask, raw, same_b, cross_b)
    return call(
        scale_final,
        "scale_final",
        jax.ShapeDtypeStruct((fine, 128, 512), jnp.bfloat16),
        [SMEM_SPEC, VMEM_SPEC, VMEM_SPEC, VMEM_SPEC, HBM_SPEC],
        HBM_SPEC,
        [pltpu.VMEM((8, 128, 512), jnp.bfloat16), pltpu.SemaphoreType.DMA((8,))],
        aliases={4: 0},
    )(targets, final, sums, swap_cores(sums), out)


def solution(mesh):
    return jax.shard_map(
        on_device,
        mesh=mesh,
        in_specs=(
            P("dom", None, None, None),
            P("dom", None),
            P("dom", None, "col"),
            P("dom", None, None),
            P("dom", None),
            P("dom"),
            P("dom", "col"),
        ),
        out_specs=P("dom", None, "col"),
        check_vma=False,
    )
```

```python
import functools

import jax
import jax.numpy as jnp
from jax import lax
from jax.experimental import pallas as pl
from jax.experimental.pallas import tpu as pltpu
from jax.sharding import PartitionSpec as P

G = 4
LEVELS = 4
GROUPS = 2
CHUNK = 8
WAVES = ((3, 1), (0, 2))
COSTS = dict(products0=1, products1=1, inner8=1, inner32=1, scale0=1, first=1, last=1)
epsilon = 1e-06
VMEM_SCOPED = 14 * 2**20
SMEM_SPEC = pl.BlockSpec(memory_space=pltpu.SMEM)
VMEM_SPEC = pl.BlockSpec(memory_space=pltpu.VMEM)
HBM_SPEC = pl.BlockSpec(memory_space=pltpu.HBM)
ANY_SPEC = pl.BlockSpec(memory_space=pl.ANY)


def lanes():
    return lax.broadcasted_iota(jnp.int32, (128, 128), 1)


def level_of(wave, core):
    first, second = WAVES[wave]
    return jnp.where(core == 0, first, second)


def row_sums(block, weights):
    full = kept = None
    for column in range(4):
        part = jnp.abs(block[:, column * 128 : (column + 1) * 128])
        weighted = part * weights[column]
        full = part if full is None else full + part
        kept = weighted if kept is None else kept + weighted
    return jnp.sum(full, axis=1, keepdims=True), jnp.sum(kept, axis=1, keepdims=True)


def weights_of(mask, block):
    return [mask[column, block].astype(jnp.float32) for column in range(4)]


def inner_block(ids, mask, block, first, second, raw, sums):
    left = jnp.concatenate([first[k] for k in range(4)], axis=1)
    right = jnp.concatenate([second[ids[k, block]] for k in range(4)], axis=0)
    product = jnp.dot(left, right, preferred_element_type=jnp.float32)
    raw[block] = product
    full, kept = row_sums(product, weights_of(mask, block))
    lane = lanes()
    sums[...] = jnp.where(lane == block, full, jnp.where(lane == block + 64, kept, sums[...]))


def tile_copy(wave, by_level, out, sem):
    return pltpu.make_async_copy(by_level.at[level_of(wave, lax.axis_index("col"))], out, sem)


def pick_tiles(by_level, out, sem):
    copy = tile_copy(0, by_level, out, sem)
    copy.start()
    copy.wait()


def inner_head(
    count,
    tables_hbm,
    first_hbm,
    second_hbm,
    by_level,
    after,
    tables,
    raw,
    sums,
    second,
    tiles_b,
    first,
    table_sem,
    first_sem,
    second_sem,
    tile_sem,
):
    del after
    ids, mask = tables[:2]
    copies = [pltpu.make_async_copy(second_hbm, second, second_sem)]
    for place, (source, target) in enumerate(zip(tables_hbm, tables)):
        copies.append(pltpu.make_async_copy(source, target, table_sem.at[place]))
    copies.append(pltpu.make_async_copy(first_hbm.at[pl.ds(0, count)], first, first_sem))
    copies.append(tile_copy(1, by_level, tiles_b, tile_sem))
    for copy in copies:
        copy.start()
    sums[...] = jnp.zeros_like(sums)
    for copy in copies:
        copy.wait()

    @pl.loop(0, count // CHUNK)
    def _(chunk):
        for j in range(CHUNK):
            block = chunk * CHUNK + j
            inner_block(ids, mask, block, first.at[block], second, raw, sums)


def inner_rest(start, count, fresh, ids, mask, first, second, raw_in, sums_in, after, raw, sums, done):
    del raw_in, after
    done[...] = jnp.zeros_like(done)
    sums[...] = jnp.zeros_like(sums) if fresh else sums_in[...]

    @pl.loop(0, count // CHUNK)
    def _(chunk):
        for j in range(CHUNK):
            block = start + chunk * CHUNK + j
            inner_block(ids, mask, block, first.at[block], second, raw, sums)


def coupling_products(wave, send_rows, tiles, second, second_other, after, out_own, out_other):
    del after
    level = level_of(wave, lax.axis_index("col"))
    for group in range(GROUPS):
        left = jnp.concatenate([tiles[group * G + s] for s in range(G)], axis=1)
        for rows, out in ((second, out_own), (second_other, out_other)):
            right = jnp.concatenate([rows[send_rows[level, group * G + s]] for s in range(G)], axis=0)
            product = jnp.dot(left, right, preferred_element_type=jnp.float32)
            top = jnp.max(jnp.abs(product), axis=1, keepdims=True)
            power = jnp.floor(jnp.log(jnp.maximum(top, 2.0**-100)) * 1.4426950408889634) + 1.0
            scaled = jnp.round(product * jnp.exp2(15.0 - power))
            coded = jnp.clip(scaled, -32767.0, 32767.0).astype(jnp.int32).astype(jnp.int16)
            for column in range(4):
                out[pl.ds((group * 4 + column) * 128, 128), :] = coded[:, column * 128 : (column + 1) * 128]
            turned = jnp.broadcast_to(power, (128, 128)).T
            out[pl.ds(1024 + 16 * group, 16), :] = turned[:16].astype(jnp.int32).astype(jnp.int16)


def scale_of(sums, sums_other):
    both = sums[...] + sums_other[...]
    scale = both[:, :64] / (both[:, 64:] + epsilon)
    return jnp.concatenate([scale, scale], axis=1)


def scale_part(start, mask, raw, sums, sums_other, out_in, after, out_hbm, done, out, sem):
    del out_in, after
    done[...] = jnp.zeros_like(done)
    scale = scale_of(sums, sums_other)

    def out_copy(chunk):
        span = pl.ds(chunk * CHUNK, CHUNK)
        return pltpu.make_async_copy(out.at[span], out_hbm.at[pl.ds(start + chunk * CHUNK, CHUNK)], sem.at[chunk])

    chunks = out.shape[0] // CHUNK

    @pl.loop(0, chunks)
    def _(chunk):
        for j in range(CHUNK):
            place = chunk * CHUNK + j
            block = start + place
            factor = jnp.take_along_axis(scale, jnp.full((128, 128), block, jnp.int32), axis=1)
            weights = weights_of(mask, block)
            for column in range(4):
                span = slice(column * 128, (column + 1) * 128)
                out[place, :, span] = (raw[block, :, span] * (factor * weights[column])).astype(jnp.bfloat16)
        out_copy(chunk).start()

    for chunk in range(chunks):
        out_copy(chunk).wait()


def add_part(targets, level, group, source, part, raw):
    block = targets[level * GROUPS + group]
    power = source[pl.ds(1024 + 16 * part, 16), :].astype(jnp.int32).astype(jnp.float32)
    step = jnp.exp2(jnp.concatenate([power] * 8, axis=0).T - 15.0)
    for column in range(4):
        span = slice(column * 128, (column + 1) * 128)
        coded = source[pl.ds((part * 4 + column) * 128, 128), :].astype(jnp.int32)
        raw[block, :, span] += coded.astype(jnp.float32) * step


def entries(wave):
    return [level * GROUPS + group for level in sorted(WAVES[wave]) for group in range(GROUPS)]


ORDER = entries(0) + entries(1)


def add_wave(wave, targets, mask, same, cross, raw, found):
    core = lax.axis_index("col")
    for group in range(GROUPS):
        add_part(targets, level_of(wave, core), group, same, group, raw)
        add_part(targets, level_of(wave, 1 - core), group, cross, group, raw)
    lane = lanes()
    for entry in entries(wave):
        block = targets[entry]
        full, kept = row_sums(raw[block], weights_of(mask, block))
        place = ORDER.index(entry)
        found = jnp.where(lane == place, full, jnp.where(lane == place + 64, kept, found))
    return found


def add_first(targets, mask, raw_in, same, cross, after, raw, sums):
    del raw_in, after
    sums[...] = add_wave(0, targets, mask, same, cross, raw, jnp.zeros((128, 128), jnp.float32))


def add_last(targets, mask, raw_in, same, cross, sums_in, raw, sums):
    del raw_in
    sums[...] = add_wave(1, targets, mask, same, cross, raw, sums_in[...])


def scale_final(targets, mask, raw, sums, sums_other, out_in, out_hbm, out, sem):
    del out_in
    scale = scale_of(sums, sums_other)
    blocks = [targets[entry] for entry in ORDER]
    latest = []
    for place, block in enumerate(blocks):
        again = jnp.bool_(False)
        for later in blocks[place + 1 :]:
            again = again | (later == block)
        latest.append(jnp.logical_not(again))

    def out_copy(place):
        return pltpu.make_async_copy(out.at[place], out_hbm.at[blocks[place]], sem.at[place])

    for place, block in enumerate(blocks):
        factor = jnp.broadcast_to(scale[:, place : place + 1], (128, 128))
        weights = weights_of(mask, block)
        for column in range(4):
            span = slice(column * 128, (column + 1) * 128)
            out[place, :, span] = (raw[block, :, span] * (factor * weights[column])).astype(jnp.bfloat16)
        pl.when(latest[place])(lambda place=place: out_copy(place).start())
    for place in range(len(blocks)):
        pl.when(latest[place])(lambda place=place: out_copy(place).wait())


def call(kernel, name, outs, in_specs, out_specs, scratch=(), aliases=None, flops=1):
    return pl.pallas_call(
        kernel,
        out_shape=outs,
        in_specs=in_specs,
        out_specs=out_specs,
        scratch_shapes=list(scratch),
        input_output_aliases=aliases or {},
        compiler_params=pltpu.CompilerParams(vmem_limit_bytes=VMEM_SCOPED),
        cost_estimate=pl.CostEstimate(flops=flops, bytes_accessed=1, transcendentals=0),
        name=name,
    )


def route(count, wave, swap):
    pairs = []
    for domain in range(count):
        for core in range(2):
            other = domain ^ (1 << WAVES[wave][core])
            pairs.append((domain * 2 + core, other * 2 + (core ^ swap)))
    return pairs


def in_hbm(array):
    return pltpu.with_memory_space_constraint(array, pltpu.HBM)


def in_vmem(array):
    return pltpu.with_memory_space_constraint(array, pltpu.VMEM)


def swap_cores(block):
    return lax.ppermute(block, "col", [(0, 1), (1, 0)])


def on_device(first_interp, first_ids, second_interp, coupling, send_rows, targets, keep_mask):
    fine = first_interp.shape[0]
    cuts = 8, 32
    count = lax.axis_size("dom")
    token = pltpu.VMEM((8, 128), jnp.float32)
    raw_shape = pltpu.VMEM((fine, 128, 512), jnp.float32)
    sums_shape = pltpu.VMEM((128, 128), jnp.float32)

    by_level = in_hbm(coupling.reshape(LEVELS, 8, 128, 128))
    tile_shape = pltpu.VMEM((8, 128, 128), jnp.bfloat16)
    tiles_a = call(pick_tiles, "pick_tiles", tile_shape, [HBM_SPEC], VMEM_SPEC, [pltpu.SemaphoreType.DMA])(by_level)
    second_other = swap_cores(second_interp)

    first = in_vmem(first_interp)
    tables = [in_hbm(x) for x in (first_ids.T, keep_mask.T, send_rows, targets)]
    head = cuts[0]
    tables, raw, sums, second, tiles_b = call(
        functools.partial(inner_head, head),
        "inner_head",
        (
            [pltpu.SMEM(x.shape, x.dtype) for x in tables],
            raw_shape,
            sums_shape,
            pltpu.VMEM((8, 128, 512), jnp.bfloat16),
            tile_shape,
        ),
        [[HBM_SPEC] * 4, HBM_SPEC, HBM_SPEC, HBM_SPEC, VMEM_SPEC],
        ([SMEM_SPEC] * 4,) + (VMEM_SPEC,) * 4,
        [
            pltpu.VMEM((head, 4, 128, 128), jnp.bfloat16),
            pltpu.SemaphoreType.DMA((4,)),
            pltpu.SemaphoreType.DMA,
            pltpu.SemaphoreType.DMA,
            pltpu.SemaphoreType.DMA,
        ],
    )(tables, in_hbm(first_interp), in_hbm(second_interp), by_level, tiles_a)
    came = [
        lax.ppermute(own, ("dom", "col"), route(count, wave, 0)) for wave, own in enumerate((tiles_a, tiles_b))
    ]
    ids, mask, send_rows, targets = tables

    def inner_part(start, stop, raw, sums, after, fresh=False):
        return call(
            functools.partial(inner_rest, start, stop - start, fresh),
            "inner_rest",
            (raw_shape, sums_shape, token),
            [SMEM_SPEC, SMEM_SPEC, VMEM_SPEC, VMEM_SPEC, VMEM_SPEC, VMEM_SPEC, VMEM_SPEC],
            (VMEM_SPEC,) * 3,
            aliases={4: 0} if fresh else {4: 0, 5: 1},
            flops=COSTS[f"inner{start}"],
        )(ids, mask, first, second, raw, sums, after)

    def products(wave, after):
        outs = call(
            functools.partial(coupling_products, wave),
            "coupling_products",
            (pltpu.VMEM((1056, 128), jnp.int16),) * 2,
            [SMEM_SPEC, VMEM_SPEC, VMEM_SPEC, VMEM_SPEC, VMEM_SPEC],
            (VMEM_SPEC,) * 2,
            flops=COSTS[f"products{wave}"],
        )(send_rows, came[wave], second, second_other, after)
        return outs, [lax.ppermute(x, ("dom", "col"), route(count, wave, swap)) for swap, x in enumerate(outs)]

    def scaled(start, stop, sums, out, after):
        return call(
            functools.partial(scale_part, start),
            "scale_part",
            (jax.ShapeDtypeStruct((fine, 128, 512), jnp.bfloat16), token),
            [SMEM_SPEC, VMEM_SPEC, VMEM_SPEC, VMEM_SPEC, HBM_SPEC if start else VMEM_SPEC, VMEM_SPEC],
            (HBM_SPEC, VMEM_SPEC),
            [pltpu.VMEM((stop - start, 128, 512), jnp.bfloat16), pltpu.SemaphoreType.DMA(((stop - start) // CHUNK,))],
            aliases={4: 0} if start else None,
            flops=COSTS[f"scale{start}"],
        )(mask, raw, sums, swap_cores(sums), out, after)

    raw, sums, done = inner_part(cuts[0], cuts[1], raw, sums, second)
    outs, (same_a, cross_a) = products(0, done)
    outs, (same_b, cross_b) = products(1, outs[0])
    raw, sums, done = inner_part(cuts[1], fine, raw, sums, outs[0])
    out, done = scaled(0, fine, sums, done, done)
    raw, sums = call(
        add_first,
        "add_first",
        (raw_shape, sums_shape),
        [SMEM_SPEC, SMEM_SPEC] + [VMEM_SPEC] * 4,
        (VMEM_SPEC,) * 2,
        aliases={2: 0},
        flops=COSTS["first"],
    )(targets, mask, raw, same_a, cross_a, done)
    raw, sums = call(
        add_last,
        "add_last",
        (raw_shape, sums_shape),
        [SMEM_SPEC, SMEM_SPEC] + [VMEM_SPEC] * 4,
        (VMEM_SPEC,) * 2,
        aliases={2: 0, 5: 1},
        flops=COSTS["last"],
    )(targets, mask, raw, same_b, cross_b, sums)
    return call(
        scale_final,
        "scale_final",
        jax.ShapeDtypeStruct((fine, 128, 512), jnp.bfloat16),
        [SMEM_SPEC, SMEM_SPEC, VMEM_SPEC, VMEM_SPEC, VMEM_SPEC, HBM_SPEC],
        HBM_SPEC,
        [pltpu.VMEM((8, 128, 512), jnp.bfloat16), pltpu.SemaphoreType.DMA((8,))],
        aliases={5: 0},
    )(targets, mask, raw, sums, swap_cores(sums), out)


def solution(mesh):
    return jax.shard_map(
        on_device,
        mesh=mesh,
        in_specs=(
            P("dom", None, None, None),
            P("dom", None),
            P("dom", None, "col"),
            P("dom", None, None),
            P("dom", None),
            P("dom"),
            P("dom", "col"),
        ),
        out_specs=P("dom", None, "col"),
        check_vma=False,
    )
```
